512 devices in a mesh: snap: 16 (over y_lo, x, core), space: 32 (over z, y_hi).
Axes of the slice: x: 4, y: 8 (y_hi: 4, y_lo: 2; y = y_hi * 2 + y_lo), z: 8, core: 2. Of those that a mesh axis runs over, the one named last changes fastest.
Arguments:
- snapshots: bfloat16 [32768, 2048], P('space', 'snap')
- cell_weight: float32 [32768], P('space'), may hold values from 0.2 to 2
- eigvec: bfloat16 [2048, 256], replicated, may hold values from -0.125 to 0.125
- time_index: int32 [2048], replicated, may hold values from 0 to 2047, each once
Outputs:
- gram: float32 [2048, 2048], P('space', 'snap')
- modes: float32 [256, 32768], P('snap', 'space')
The draws below stay inside these ranges and needn't reach their ends.
Inputs may be any that keep to these rules, and one draw needn't show every extreme that they name: `time_index`: each value of 0 to 2047 appears exactly once.
All inputs are finite; a program needn't handle non-finite values.
Results may differ from the reference program's by a relative error of at most 0.00081.
Values may be sent and summed in bfloat16 or wider, within the bound.
No kernel may reach another device: no remote copies, remote signals or barrier semaphores. Data moves between devices by JAX's collectives and lax.ppermute only.
A program may use at most 64 MiB of HBM per device.

```python
import math
import jax
import jax.numpy as jnp
from jax import lax

MODES = 256
SNAPS = 2048
ROWS = 32768


def draw_snapshots(key, part):
    key = jax.random.fold_in(key, 11)
    key_noise, key_rows, key_cols = jax.random.split(key, 3)
    row_scale = jnp.exp(jax.random.uniform(key_rows, (ROWS, 1), jnp.float32, jnp.log(0.3), jnp.log(3.0)))
    col_scale = jnp.exp(jax.random.uniform(key_cols, (1, SNAPS), jnp.float32, jnp.log(0.3), jnp.log(3.0)))
    noise = jax.random.normal(key_noise, (ROWS, SNAPS), jnp.float32)
    values = jnp.clip(noise, -5.0, 5.0) * row_scale * col_scale
    return values.astype(jnp.bfloat16)


def steps_of(key, shape, cuts, least, high):
    level = 1.0
    for position, shards_of in cuts:
        steps = jax.random.uniform(jax.random.fold_in(jax.random.fold_in(key, 6), position), (shards_of,), jnp.float32, least / len(cuts), high / len(cuts))
        level = level * jnp.repeat(jnp.exp(steps), shape[position] // shards_of).reshape((-1,) + (1,) * (len(shape) - 1 - position))
    return level


def centred(own_key, dims, scale, limit, held_as=jnp.bfloat16):
    return jnp.clip(scale * jax.random.normal(own_key, dims, jnp.float32), -limit, limit).astype(held_as)


def setup_inputs(seed: int = 0) -> dict:
    keys = jax.random.split(jax.random.key(seed), 5)
    snapshots = draw_snapshots(jax.random.fold_in(keys[4], 71), 0)
    cell_weight = jnp.clip(jnp.exp(math.log(2.0) - 2.3025851 * jax.random.uniform(keys[1], (ROWS,), jnp.float32) ** steps_of(keys[1], (ROWS,), ((0, 32),), -0.2, 0.2)), 0.2, 2.0)
    eigvec = centred(keys[2], (SNAPS, MODES), SNAPS ** -0.5, 0.125)
    time_index = jax.random.permutation(keys[3], SNAPS).astype(jnp.int32)
    return {"snapshots": snapshots, "cell_weight": cell_weight, "eigvec": eigvec, "time_index": time_index}


def reference(snapshots, cell_weight, eigvec, time_index):
    weighted = (snapshots.astype(jnp.float32) * cell_weight[:, None]).astype(jnp.bfloat16)
    gram = lax.dot_general(snapshots, weighted, (((0,), (0,)), ((), ())), preferred_element_type=jnp.float32)
    gram = gram / ROWS
    ordered = jnp.take(eigvec, time_index.astype(jnp.int32), axis=0)
    modes = lax.dot_general(ordered, snapshots, (((0,), (1,)), ((), ())), preferred_element_type=jnp.float32)
    return gram, modes
```

```python
import jax
import jax.numpy as jnp
from jax import lax
from jax.experimental import pallas as pl
from jax.experimental.pallas import tpu as pltpu
from jax.sharding import Mesh, PartitionSpec as P

SWAP = [(0, 1), (1, 0)]


def gram_kernel(same_ref, other_ref, weighted_ref, out_ref):
    core = lax.axis_index("core")
    weighted = weighted_ref[...]
    for rows_ref, core1 in ((same_ref, core), (other_ref, 1 - core)):
        for x1 in range(4):
            part = lax.dot_general(
                rows_ref[x1], weighted, (((0,), (0,)), ((), ())), preferred_element_type=jnp.float32
            ).astype(jnp.bfloat16)
            for y2 in range(2):
                for half in range(2):
                    out_ref[y2 * 4 + core1 * 2 + half, x1] = part[
                        half * 64 : half * 64 + 64, y2 * 128 : y2 * 128 + 128
                    ]


def modes_kernel(same_ref, other_ref, ordered_ref, out_ref):
    core = lax.axis_index("core")
    total = jnp.zeros(out_ref.shape, jnp.float32)
    for rows_ref, core1 in ((same_ref, core), (other_ref, 1 - core)):
        for x1 in range(4):
            total += lax.dot_general(
                ordered_ref[core1, x1], rows_ref[x1], (((1,), (1,)), ((), ())), preferred_element_type=jnp.float32
            )
    out_ref[...] = total


def body(snapshots, cell_weight, eigvec, time_index):
    rows, width = snapshots.shape
    y, x, core = lax.axis_index("yl"), lax.axis_index("x"), lax.axis_index("core")
    scaling = 1.0 / (rows * lax.axis_size("z") * lax.axis_size("yh"))

    partner = lax.ppermute(snapshots, "yl", SWAP)
    same = lax.all_to_all(jnp.broadcast_to(snapshots[None], (4, rows, width)), "x", 0, 0, tiled=True)
    same, partner = lax.optimization_barrier((same, partner))
    other = lax.ppermute(same, "core", SWAP)

    index = lax.dynamic_slice_in_dim(time_index, y * 1024, 1024, 0)
    ordered = jnp.take(eigvec, index, axis=0)
    ordered = ordered.reshape(4, 2, 128, 2, 8, 16)
    ordered = lax.dynamic_index_in_dim(ordered, x * 2 + core, 4, keepdims=False)
    ordered = ordered.transpose(1, 0, 3, 4, 2).reshape(2, 4, 32, 128)

    first = jnp.where(y == 0, snapshots, partner).astype(jnp.float32)
    second = jnp.where(y == 0, partner, snapshots).astype(jnp.float32)
    weighted = (jnp.concatenate([first, second], 1) * cell_weight[:, None]).astype(jnp.bfloat16)

    vmem = pl.BlockSpec(memory_space=pltpu.VMEM)
    parts = pl.pallas_call(
        gram_kernel,
        out_shape=jax.ShapeDtypeStruct((8, 4, 64, 128), jnp.bfloat16),
        in_specs=[vmem] * 3,
        out_specs=vmem,
        compiler_params=pltpu.CompilerParams(vmem_limit_bytes=32 * 1024 * 1024),
        name="gram_parts",
    )(same, other, weighted)
    mode_part = pl.pallas_call(
        modes_kernel,
        out_shape=jax.ShapeDtypeStruct((32, rows), jnp.float32),
        in_specs=[vmem] * 3,
        out_specs=vmem,
        compiler_params=pltpu.CompilerParams(vmem_limit_bytes=32 * 1024 * 1024),
        name="mode_parts",
    )(same, other, ordered)

    parts = lax.all_to_all(parts, ("yl", "yh"), 0, 0, tiled=True)
    mode_part = mode_part.reshape(2, 16, rows)
    away = lax.ppermute(lax.dynamic_index_in_dim(mode_part, 1 - y, 0, keepdims=False), "yl", SWAP)
    modes = lax.dynamic_index_in_dim(mode_part, y, 0, keepdims=False) + away

    parts = jnp.sum(parts.reshape(2, 4, 4, 64, 128).astype(jnp.float32), axis=1)
    parts = lax.all_to_all(parts.reshape(8, 64, 128), "z", 0, 0, tiled=True)
    gram = jnp.sum(parts, axis=0) * scaling
    return gram, modes


def solution(mesh):
    fine = Mesh(mesh.devices.reshape(2, 4, 2, 8, 4), ("yl", "x", "core", "z", "yh"))
    snap, space = ("yl", "x", "core"), ("z", "yh")
    in_specs = (P(space, snap), P(space), P(), P())
    out_specs = (P(space, snap), P(snap, space))
    return jax.shard_map(body, mesh=fine, in_specs=in_specs, out_specs=out_specs, check_vma=False)
```

```python
import jax
import jax.numpy as jnp
from jax import lax
from jax.experimental import pallas as pl
from jax.experimental.pallas import tpu as pltpu
from jax.sharding import Mesh, PartitionSpec as P

SWAP = [(0, 1), (1, 0)]
VMEM = pl.BlockSpec(memory_space=pltpu.VMEM)


def local(kernel, out_shape, *operands, name):
    outs = jax.tree.map(lambda _: VMEM, out_shape)
    return pl.pallas_call(
        kernel,
        out_shape=out_shape,
        in_specs=[VMEM] * len(operands),
        out_specs=outs,
        compiler_params=pltpu.CompilerParams(vmem_limit_bytes=32 * 1024 * 1024),
        name=name,
    )(*operands)


def ordered_kernel(index_ref, eigvec_ref, out_ref):
    y, x, core = lax.axis_index("yl"), lax.axis_index("x"), lax.axis_index("core")
    times, modes = eigvec_ref.shape
    row = lax.broadcasted_iota(jnp.int32, (32, modes), 0)
    column = lax.broadcasted_iota(jnp.int32, (32, modes), 1)
    wanted = (row // 16) * 128 + (x * 2 + core) * 16 + row % 16
    chosen = (column == wanted).astype(jnp.float32).astype(jnp.bfloat16)
    kept = lax.dot_general(
        chosen, eigvec_ref[...], (((1,), (1,)), ((), ())), preferred_element_type=jnp.float32
    ).astype(jnp.bfloat16)
    time = lax.broadcasted_iota(jnp.int32, (times, 128), 0)
    for x1 in range(4):
        for core1 in range(2):
            index = index_ref[pl.ds(y * 8 + x1 * 2 + core1, 1), :]
            hot = (time == index).astype(jnp.float32).astype(jnp.bfloat16)
            out_ref[core1, x1] = jnp.dot(kept, hot, preferred_element_type=jnp.float32).astype(jnp.bfloat16)


def shifts():
    x = lax.axis_index("x")
    return x, (x + 3) % 4, (x + 1) % 4, (x + 2) % 4


def stack_kernel(*refs):
    for k, block in enumerate(refs[:-1]):
        refs[-1][k] = block[...]


def gram_blocks(rows_ref, weighted_ref, store):
    weighted = weighted_ref[...]
    for k in range(4):
        part = lax.dot_general(
            rows_ref[k], weighted, (((0,), (0,)), ((), ())), preferred_element_type=jnp.float32
        ).astype(jnp.bfloat16)
        for side in range(2):
            for half in range(2):
                store(side, half, k, part[half * 64 : half * 64 + 64, side * 128 : side * 128 + 128])


def gram_same_kernel(rows_ref, weighted_ref, out_ref):
    def store(side, half, k, tile):
        out_ref[side * 2 + half, k] = tile

    gram_blocks(rows_ref, weighted_ref, store)


def gram_other_kernel(rows_ref, weighted_ref, begun_ref, out_ref):
    y, core = lax.axis_index("yl"), lax.axis_index("core")
    places = shifts()

    def place(side, half, core1):
        return (y if side == 0 else 1 - y) * 4 + core1 * 2 + half

    for k in range(4):
        for side in range(2):
            for half in range(2):
                out_ref[place(side, half, core), places[k]] = begun_ref[side * 2 + half, k]

    def store(side, half, k, tile):
        out_ref[place(side, half, 1 - core), places[k]] = tile

    gram_blocks(rows_ref, weighted_ref, store)


def modes_blocks(rows_ref, ordered_ref, core1):
    total = None
    for k, x1 in enumerate(shifts()):
        part = lax.dot_general(
            ordered_ref[core1, x1], rows_ref[k], (((1,), (1,)), ((), ())), preferred_element_type=jnp.float32
        )
        total = part if total is None else total + part
    return total


def modes_same_kernel(rows_ref, ordered_ref, out_ref):
    out_ref[...] = modes_blocks(rows_ref, ordered_ref, lax.axis_index("core"))


def modes_other_kernel(rows_ref, ordered_ref, begun_ref, away_ref, stay_ref):
    total = begun_ref[...] + modes_blocks(rows_ref, ordered_ref, 1 - lax.axis_index("core"))
    first = lax.axis_index("yl") == 0
    stay_ref[...] = jnp.where(first, total[:16], total[16:])
    away_ref[...] = jnp.where(first, total[16:], total[:16])


def sum_kernel(scaling, parts_ref, out_ref):
    for y1 in range(2):
        for x1 in range(4):
            total = parts_ref[y1 * 4, x1].astype(jnp.float32)
            for k in range(1, 4):
                total += parts_ref[y1 * 4 + k, x1].astype(jnp.float32)
            out_ref[y1 * 4 + x1] = total * scaling


def last_kernel(parts_ref, stay_ref, away_ref, gram_ref, modes_ref):
    total = parts_ref[0]
    for k in range(1, 8):
        total += parts_ref[k]
    gram_ref[...] = total
    modes_ref[...] = stay_ref[...] + away_ref[...]


def body(snapshots, cell_weight, eigvec, time_index):
    rows, width = snapshots.shape
    scaling = 1.0 / (rows * lax.axis_size("z") * lax.axis_size("yh"))
    shape = jax.ShapeDtypeStruct

    def shift(k):
        return lax.ppermute(snapshots, "x", [(i, (i + k) % 4) for i in range(4)])

    across, ahead, behind = shift(2), shift(1), shift(3)
    partner = lax.ppermute(snapshots, "yl", SWAP)
    weighted = (jnp.concatenate([snapshots, partner], 1).astype(jnp.float32) * cell_weight[:, None]).astype(
        jnp.bfloat16
    )
    ordered = local(
        ordered_kernel, shape((2, 4, 32, 128), jnp.bfloat16), time_index.reshape(16, 128), eigvec, name="ordered"
    )
    across, ahead, behind, weighted, ordered = lax.optimization_barrier((across, ahead, behind, weighted, ordered))
    stacked = shape((4, rows, width), jnp.bfloat16)
    same = local(stack_kernel, stacked, snapshots, ahead, behind, across, name="stack")
    other = lax.ppermute(same, "core", SWAP)
    begun = local(gram_same_kernel, shape((4, 4, 64, 128), jnp.bfloat16), same, weighted, name="gram_same")
    modes = local(modes_same_kernel, shape((32, rows), jnp.float32), same, ordered, name="modes_same")
    other, begun, modes = lax.optimization_barrier((other, begun, modes))
    parts = local(
        gram_other_kernel, shape((8, 4, 64, 128), jnp.bfloat16), other, weighted, begun, name="gram_other"
    )
    parts = lax.all_to_all(parts, ("yl", "yh"), 0, 0, tiled=True)
    parts = local(lambda *refs: sum_kernel(scaling, *refs), shape((8, 64, 128), jnp.float32), parts, name="sum_y")
    parts, other, ordered, modes = lax.optimization_barrier((parts, other, ordered, modes))
    parts = lax.all_to_all(parts, "z", 0, 0, tiled=True)
    half = shape((16, rows), jnp.float32)
    away, stay = local(modes_other_kernel, [half, half], other, ordered, modes, name="modes_other")
    away = lax.ppermute(away, "yl", SWAP)
    outs = [shape((64, 128), jnp.float32), half]
    gram, modes = local(last_kernel, outs, parts, stay, away, name="sum_z")
    return gram, modes


def solution(mesh):
    fine = Mesh(mesh.devices.reshape(2, 4, 2, 8, 4), ("yl", "x", "core", "z", "yh"))
    snap, space = ("yl", "x", "core"), ("z", "yh")
    in_specs = (P(space, snap), P(space), P(), P())
    out_specs = (P(space, snap), P(snap, space))
    return jax.shard_map(body, mesh=fine, in_specs=in_specs, out_specs=out_specs, check_vma=False)
```

```python
import jax
import jax.numpy as jnp
from jax import lax
from jax.experimental import pallas as pl
from jax.experimental.pallas import tpu as pltpu
from jax.sharding import Mesh, PartitionSpec as P

SWAP = [(0, 1), (1, 0)]
HIDE = 20 * 10**9
VMEM = pl.BlockSpec(memory_space=pltpu.VMEM)


def local(kernel, out_shape, *operands, name, flops=0):
    outs = jax.tree.map(lambda _: VMEM, out_shape)
    return pl.pallas_call(
        kernel,
        out_shape=out_shape,
        in_specs=[VMEM] * len(operands),
        out_specs=outs,
        compiler_params=pltpu.CompilerParams(vmem_limit_bytes=32 * 1024 * 1024),
        cost_estimate=pl.CostEstimate(flops=flops, bytes_accessed=0, transcendentals=0) if flops else None,
        name=name,
    )(*operands)


def ordered_kernel(index_ref, eigvec_ref, out_ref):
    y, x, core = lax.axis_index("yl"), lax.axis_index("x"), lax.axis_index("core")
    times, modes = eigvec_ref.shape
    row = lax.broadcasted_iota(jnp.int32, (32, modes), 0)
    column = lax.broadcasted_iota(jnp.int32, (32, modes), 1)
    wanted = (row // 16) * 128 + (x * 2 + core) * 16 + row % 16
    chosen = (column == wanted).astype(jnp.float32).astype(jnp.bfloat16)
    kept = lax.dot_general(
        chosen, eigvec_ref[...], (((1,), (1,)), ((), ())), preferred_element_type=jnp.float32
    ).astype(jnp.bfloat16)
    time = lax.broadcasted_iota(jnp.int32, (times, 128), 0)
    for x1 in range(4):
        for core1 in range(2):
            index = index_ref[pl.ds(y * 8 + x1 * 2 + core1, 1), :]
            hot = (time == index).astype(jnp.float32).astype(jnp.bfloat16)
            out_ref[core1, x1] = jnp.dot(kept, hot, preferred_element_type=jnp.float32).astype(jnp.bfloat16)


def shifts():
    x = lax.axis_index("x")
    return x, (x + 3) % 4, (x + 1) % 4, (x + 2) % 4


def stack_kernel(*refs):
    for k, block in enumerate(refs[:-1]):
        refs[-1][k] = block[...]


def gram_blocks(rows_ref, weighted_ref, store):
    weighted = weighted_ref[...]
    for k in range(4):
        part = lax.dot_general(
            rows_ref[k], weighted, (((0,), (0,)), ((), ())), preferred_element_type=jnp.float32
        ).astype(jnp.bfloat16)
        for side in range(2):
            for half in range(2):
                store(side, half, k, part[half * 64 : half * 64 + 64, side * 128 : side * 128 + 128])


def gram_same_kernel(rows_ref, weighted_ref, out_ref):
    def store(side, half, k, tile):
        out_ref[side * 2 + half, k] = tile

    gram_blocks(rows_ref, weighted_ref, store)


def gram_other_kernel(rows_ref, weighted_ref, begun_ref, out_ref):
    y, core = lax.axis_index("yl"), lax.axis_index("core")
    places = shifts()

    def place(side, half, core1):
        return (y if side == 0 else 1 - y) * 4 + core1 * 2 + half

    for k in range(4):
        for side in range(2):
            for half in range(2):
                out_ref[place(side, half, core), places[k]] = begun_ref[side * 2 + half, k]

    def store(side, half, k, tile):
        out_ref[place(side, half, 1 - core), places[k]] = tile

    gram_blocks(rows_ref, weighted_ref, store)


def modes_blocks(rows_ref, ordered_ref, core1):
    total = None
    for k, x1 in enumerate(shifts()):
        part = lax.dot_general(
            ordered_ref[core1, x1], rows_ref[k], (((1,), (1,)), ((), ())), preferred_element_type=jnp.float32
        )
        total = part if total is None else total + part
    return total


def modes_same_kernel(rows_ref, ordered_ref, out_ref):
    out_ref[...] = modes_blocks(rows_ref, ordered_ref, lax.axis_index("core"))


def modes_other_kernel(rows_ref, ordered_ref, begun_ref, away_ref, stay_ref):
    total = begun_ref[...] + modes_blocks(rows_ref, ordered_ref, 1 - lax.axis_index("core"))
    first = lax.axis_index("yl") == 0
    stay_ref[...] = jnp.where(first, total[:16], total[16:])
    away_ref[...] = jnp.where(first, total[16:], total[:16])


def sum_kernel(scaling, parts_ref, out_ref):
    for y1 in range(2):
        for x1 in range(4):
            total = parts_ref[y1 * 4, x1].astype(jnp.float32)
            for k in range(1, 4):
                total += parts_ref[y1 * 4 + k, x1].astype(jnp.float32)
            out_ref[y1 * 4 + x1] = total * scaling


def last_kernel(parts_ref, stay_ref, away_ref, gram_ref, modes_ref):
    total = parts_ref[0]
    for k in range(1, 8):
        total += parts_ref[k]
    gram_ref[...] = total
    modes_ref[...] = stay_ref[...] + away_ref[...]


def body(snapshots, cell_weight, eigvec, time_index):
    rows, width = snapshots.shape
    scaling = 1.0 / (rows * lax.axis_size("z") * lax.axis_size("yh"))
    shape = jax.ShapeDtypeStruct

    def shift(k):
        return lax.ppermute(snapshots, "x", [(i, (i + k) % 4) for i in range(4)])

    across, ahead, behind = shift(2), shift(1), shift(3)
    partner = lax.ppermute(snapshots, "yl", SWAP)
    ordered = local(
        ordered_kernel, shape((2, 4, 32, 128), jnp.bfloat16), time_index.reshape(16, 128), eigvec, name="ordered"
    )
    across, ahead, behind, ordered = lax.optimization_barrier((across, ahead, behind, ordered))
    stacked = shape((4, rows, width), jnp.bfloat16)
    same = local(stack_kernel, stacked, snapshots, ahead, behind, across, name="stack")
    other = lax.ppermute(same, "core", SWAP)
    weighted = (jnp.concatenate([snapshots, partner], 1).astype(jnp.float32) * cell_weight[:, None]).astype(
        jnp.bfloat16
    )
    begun = local(gram_same_kernel, shape((4, 4, 64, 128), jnp.bfloat16), same, weighted, name="gram_same", flops=HIDE)
    modes = local(modes_same_kernel, shape((32, rows), jnp.float32), same, ordered, name="modes_same")
    other, begun, modes = lax.optimization_barrier((other, begun, modes))
    parts = local(
        gram_other_kernel, shape((8, 4, 64, 128), jnp.bfloat16), other, weighted, begun, name="gram_other"
    )
    parts = lax.all_to_all(parts, ("yl", "yh"), 0, 0, tiled=True)
    parts = local(lambda *refs: sum_kernel(scaling, *refs), shape((8, 64, 128), jnp.float32), parts, name="sum_y")
    parts, other, ordered, modes = lax.optimization_barrier((parts, other, ordered, modes))
    parts = lax.all_to_all(parts, "z", 0, 0, tiled=True)
    half = shape((16, rows), jnp.float32)
    away, stay = local(modes_other_kernel, [half, half], other, ordered, modes, name="modes_other")
    away = lax.ppermute(away, "yl", SWAP)
    outs = [shape((64, 128), jnp.float32), half]
    gram, modes = local(last_kernel, outs, parts, stay, away, name="sum_z")
    return gram, modes


def solution(mesh):
    fine = Mesh(mesh.devices.reshape(2, 4, 2, 8, 4), ("yl", "x", "core", "z", "yh"))
    snap, space = ("yl", "x", "core"), ("z", "yh")
    in_specs = (P(space, snap), P(space), P(), P())
    out_specs = (P(space, snap), P(snap, space))
    return jax.shard_map(body, mesh=fine, in_specs=in_specs, out_specs=out_specs, check_vma=False)
```

```python
import jax
import jax.numpy as jnp
from jax import lax
from jax.experimental import pallas as pl
from jax.experimental.pallas import tpu as pltpu
from jax.sharding import Mesh, PartitionSpec as P

SWAP = [(0, 1), (1, 0)]
HIDE = 20 * 10**9
VMEM = pl.BlockSpec(memory_space=pltpu.VMEM)


def local(kernel, out_shape, *operands, name, flops=0):
    outs = jax.tree.map(lambda _: VMEM, out_shape)
    return pl.pallas_call(
        kernel,
        out_shape=out_shape,
        in_specs=[VMEM] * len(operands),
        out_specs=outs,
        compiler_params=pltpu.CompilerParams(vmem_limit_bytes=32 * 1024 * 1024),
        cost_estimate=pl.CostEstimate(flops=flops, bytes_accessed=0, transcendentals=0) if flops else None,
        name=name,
    )(*operands)


def ordered_kernel(index_ref, eigvec_ref, out_ref):
    y, x, core = lax.axis_index("yl"), lax.axis_index("x"), lax.axis_index("core")
    times, modes = eigvec_ref.shape
    row = lax.broadcasted_iota(jnp.int32, (32, modes), 0)
    column = lax.broadcasted_iota(jnp.int32, (32, modes), 1)
    wanted = (row // 16) * 128 + (x * 2 + core) * 16 + row % 16
    chosen = (column == wanted).astype(jnp.float32).astype(jnp.bfloat16)
    kept = lax.dot_general(
        chosen, eigvec_ref[...], (((1,), (1,)), ((), ())), preferred_element_type=jnp.float32
    ).astype(jnp.bfloat16)
    time = lax.broadcasted_iota(jnp.int32, (times, 128), 0)
    for x1 in range(4):
        for core1 in range(2):
            index = index_ref[pl.ds(y * 8 + x1 * 2 + core1, 1), :]
            hot = (time == index).astype(jnp.float32).astype(jnp.bfloat16)
            out_ref[core1, x1] = jnp.dot(kept, hot, preferred_element_type=jnp.float32).astype(jnp.bfloat16)


def shifts():
    x = lax.axis_index("x")
    return x, (x + 2) % 4, (x + 3) % 4, (x + 1) % 4


def stack_kernel(first_ref, second_ref, out_ref):
    out_ref[0], out_ref[1] = first_ref[...], second_ref[...]


def gram_blocks(pair_ref, weighted_ref, store):
    weighted = weighted_ref[...]
    for k in range(2):
        part = lax.dot_general(
            pair_ref[k], weighted, (((0,), (0,)), ((), ())), preferred_element_type=jnp.float32
        ).astype(jnp.bfloat16)
        for side in range(2):
            for half in range(2):
                store(k, side * 2 + half, part[half * 64 : half * 64 + 64, side * 128 : side * 128 + 128])


def gram_begin_kernel(pairs, *refs):
    *pair_refs, weighted_ref, out_ref = refs
    for pair in range(pairs):

        def store(k, corner, tile):
            out_ref[pair * 2 + k, corner] = tile

        gram_blocks(pair_refs[pair], weighted_ref, store)


def gram_end_kernel(last_ref, weighted_ref, begun_ref, out_ref):
    y, core = lax.axis_index("yl"), lax.axis_index("core")
    places = shifts()

    def store(k, corner, tile):
        y2, core1, x1 = (y, 1 - y)[corner // 2], (core, 1 - core)[k // 4], places[k % 4]
        out_ref[y2 * 8 + x1 % 2 * 4 + core1 * 2 + corner % 2, x1 // 2] = tile

    for k in range(6):
        for corner in range(4):
            store(k, corner, begun_ref[k, corner])
    gram_blocks(last_ref, weighted_ref, lambda k, corner, tile: store(6 + k, corner, tile))


def modes_kernel(one_ref, two_ref, one_other_ref, two_other_ref, ordered_ref, away_ref, stay_ref):
    core, places = lax.axis_index("core"), shifts()
    total = jnp.zeros((32, stay_ref.shape[1]), jnp.float32)
    for refs, core1 in (((one_ref, two_ref), core), ((one_other_ref, two_other_ref), 1 - core)):
        for k, x1 in enumerate(places):
            total += lax.dot_general(
                ordered_ref[core1, x1], refs[k // 2][k % 2], (((1,), (1,)), ((), ())), preferred_element_type=jnp.float32
            )
    first = lax.axis_index("yl") == 0
    stay_ref[...] = jnp.where(first, total[:16], total[16:])
    away_ref[...] = jnp.where(first, total[16:], total[:16])


def sum_kernel(scaling, parts_ref, out_ref):
    for y1 in range(2):
        for high in range(2):
            total = parts_ref[y1 * 8, high].astype(jnp.float32)
            for k in range(1, 8):
                total += parts_ref[y1 * 8 + k, high].astype(jnp.float32)
            out_ref[y1 * 2 + high] = total * scaling


def last_kernel(parts_ref, stay_ref, away_ref, gram_ref, modes_ref):
    total = parts_ref[0]
    for k in range(1, 4):
        total += parts_ref[k]
    gram_ref[...] = total
    modes_ref[...] = stay_ref[...] + away_ref[...]


def body(snapshots, cell_weight, eigvec, time_index):
    rows, width = snapshots.shape
    scaling = 1.0 / (rows * lax.axis_size("zh") * lax.axis_size("zl") * lax.axis_size("yh"))
    shape = jax.ShapeDtypeStruct

    def shift(k):
        return lax.ppermute(snapshots, "x", [(i, (i + k) % 4) for i in range(4)])

    across, ahead, behind = shift(2), shift(1), shift(3)
    partner = lax.ppermute(snapshots, "yl", SWAP)
    pair = shape((2, rows, width), jnp.bfloat16)
    one = local(stack_kernel, pair, snapshots, across, name="stack_one")
    one_other = lax.ppermute(one, "core", SWAP)
    two = local(stack_kernel, pair, ahead, behind, name="stack_two", flops=HIDE)
    two_other = lax.ppermute(two, "core", SWAP)
    weighted = (jnp.concatenate([snapshots, partner], 1).astype(jnp.float32) * cell_weight[:, None]).astype(
        jnp.bfloat16
    )
    begun = local(
        lambda *refs: gram_begin_kernel(3, *refs),
        shape((6, 4, 64, 128), jnp.bfloat16),
        one,
        two,
        one_other,
        weighted,
        name="gram_begin",
        flops=HIDE,
    )
    two_other, begun = lax.optimization_barrier((two_other, begun))
    parts = local(
        gram_end_kernel, shape((16, 2, 64, 128), jnp.bfloat16), two_other, weighted, begun, name="gram_end"
    )
    parts = lax.all_to_all(parts, ("yl", "zl", "yh"), 0, 0, tiled=True)
    parts = local(lambda *refs: sum_kernel(scaling, *refs), shape((4, 64, 128), jnp.float32), parts, name="sum_y")
    parts, one, two, one_other, two_other, time_index, eigvec = lax.optimization_barrier(
        (parts, one, two, one_other, two_other, time_index, eigvec)
    )
    parts = lax.all_to_all(parts, "zh", 0, 0, tiled=True)
    ordered = local(
        ordered_kernel, shape((2, 4, 32, 128), jnp.bfloat16), time_index.reshape(16, 128), eigvec, name="ordered"
    )
    half = shape((16, rows), jnp.float32)
    blocks = one, two, one_other, two_other
    away, stay = local(modes_kernel, [half, half], *blocks, ordered, name="mode_parts")
    away = lax.ppermute(away, "yl", SWAP)
    outs = [shape((64, 128), jnp.float32), half]
    gram, modes = local(last_kernel, outs, parts, stay, away, name="sum_z")
    return gram, modes


def solution(mesh):
    fine = Mesh(mesh.devices.reshape(2, 4, 2, 4, 2, 4), ("yl", "x", "core", "zh", "zl", "yh"))
    snap, space = ("yl", "x", "core"), ("zh", "zl", "yh")
    in_specs = (P(space, snap), P(space), P(), P())
    out_specs = (P(space, snap), P(snap, space))
    return jax.shard_map(body, mesh=fine, in_specs=in_specs, out_specs=out_specs, check_vma=False)
```

```python
import jax
import jax.numpy as jnp
from jax import lax
from jax.experimental import pallas as pl
from jax.experimental.pallas import tpu as pltpu
from jax.sharding import Mesh, PartitionSpec as P

SWAP = [(0, 1), (1, 0)]
HIDE = 20 * 10**9
VMEM = pl.BlockSpec(memory_space=pltpu.VMEM)


def local(kernel, out_shape, *operands, name, flops=0):
    outs = jax.tree.map(lambda _: VMEM, out_shape)
    return pl.pallas_call(
        kernel,
        out_shape=out_shape,
        in_specs=[VMEM] * len(operands),
        out_specs=outs,
        compiler_params=pltpu.CompilerParams(vmem_limit_bytes=32 * 1024 * 1024),
        cost_estimate=pl.CostEstimate(flops=flops, bytes_accessed=0, transcendentals=0) if flops else None,
        name=name,
    )(*operands)


def ordered_kernel(index_ref, eigvec_ref, out_ref):
    y, x, core = lax.axis_index("yl"), lax.axis_index("x"), lax.axis_index("core")
    times, modes = eigvec_ref.shape
    row = lax.broadcasted_iota(jnp.int32, (32, modes), 0)
    column = lax.broadcasted_iota(jnp.int32, (32, modes), 1)
    wanted = (row // 16) * 128 + (x * 2 + core) * 16 + row % 16
    chosen = (column == wanted).astype(jnp.float32).astype(jnp.bfloat16)
    kept = lax.dot_general(
        chosen, eigvec_ref[...], (((1,), (1,)), ((), ())), preferred_element_type=jnp.float32
    ).astype(jnp.bfloat16)
    time = lax.broadcasted_iota(jnp.int32, (times, 128), 0)
    for x1 in range(4):
        for core1 in range(2):
            index = index_ref[pl.ds(y * 8 + x1 * 2 + core1, 1), :]
            hot = (time == index).astype(jnp.float32).astype(jnp.bfloat16)
            out_ref[core1, x1] = jnp.dot(kept, hot, preferred_element_type=jnp.float32).astype(jnp.bfloat16)


def shifts():
    x = lax.axis_index("x")
    return x, (x + 2) % 4, x + 1 - x % 2 * 2, 3 - x


def stack_kernel(first_ref, second_ref, out_ref):
    out_ref[0], out_ref[1] = first_ref[...], second_ref[...]


def gram_blocks(pair_ref, weighted_ref, store):
    weighted = weighted_ref[...]
    for k in range(2):
        part = lax.dot_general(
            pair_ref[k], weighted, (((0,), (0,)), ((), ())), preferred_element_type=jnp.float32
        ).astype(jnp.bfloat16)
        for side in range(2):
            for half in range(2):
                store(k, side * 2 + half, part[half * 64 : half * 64 + 64, side * 128 : side * 128 + 128])


def gram_begin_kernel(pairs, *refs):
    *pair_refs, weighted_ref, out_ref = refs
    for pair in range(pairs):

        def store(k, corner, tile):
            out_ref[pair * 2 + k, corner] = tile

        gram_blocks(pair_refs[pair], weighted_ref, store)


def gram_end_kernel(last_ref, weighted_ref, begun_ref, out_ref):
    y, core = lax.axis_index("yl"), lax.axis_index("core")
    places = shifts()

    def store(k, corner, tile):
        y2, core1, x1 = (y, 1 - y)[corner // 2], (core, 1 - core)[k // 4], places[k % 4]
        out_ref[y2 * 8 + x1 % 2 * 4 + core1 * 2 + corner % 2, x1 // 2] = tile

    for k in range(6):
        for corner in range(4):
            store(k, corner, begun_ref[k, corner])
    gram_blocks(last_ref, weighted_ref, lambda k, corner, tile: store(6 + k, corner, tile))


def modes_kernel(one_ref, two_ref, one_other_ref, two_other_ref, ordered_ref, away_ref, stay_ref):
    core, places = lax.axis_index("core"), shifts()
    total = jnp.zeros((32, stay_ref.shape[1]), jnp.float32)
    for refs, core1 in (((one_ref, two_ref), core), ((one_other_ref, two_other_ref), 1 - core)):
        for k, x1 in enumerate(places):
            total += lax.dot_general(
                ordered_ref[core1, x1], refs[k // 2][k % 2], (((1,), (1,)), ((), ())), preferred_element_type=jnp.float32
            )
    first = lax.axis_index("yl") == 0
    stay_ref[...] = jnp.where(first, total[:16], total[16:])
    away_ref[...] = jnp.where(first, total[16:], total[:16])


def sum_kernel(scaling, parts_ref, out_ref):
    for y1 in range(2):
        for high in range(2):
            total = parts_ref[y1 * 8, high].astype(jnp.float32)
            for k in range(1, 8):
                total += parts_ref[y1 * 8 + k, high].astype(jnp.float32)
            out_ref[y1 * 2 + high] = total * scaling


def last_kernel(parts_ref, stay_ref, away_ref, gram_ref, modes_ref):
    total = parts_ref[0]
    for k in range(1, 4):
        total += parts_ref[k]
    gram_ref[...] = total
    modes_ref[...] = stay_ref[...] + away_ref[...]


def body(snapshots, cell_weight, eigvec, time_index):
    rows, width = snapshots.shape
    scaling = 1.0 / (rows * lax.axis_size("zh") * lax.axis_size("zl") * lax.axis_size("yh"))
    shape = jax.ShapeDtypeStruct

    def trade(k):
        return lax.ppermute(snapshots, "x", [(i, i ^ k) for i in range(4)])

    across, ahead, behind = trade(2), trade(1), trade(3)
    partner = lax.ppermute(snapshots, "yl", SWAP)
    pair = shape((2, rows, width), jnp.bfloat16)
    one = local(stack_kernel, pair, snapshots, across, name="stack_one")
    one_other = lax.ppermute(one, "core", SWAP)
    two = local(stack_kernel, pair, ahead, behind, name="stack_two", flops=HIDE)
    two_other = lax.ppermute(two, "core", SWAP)
    weighted = (jnp.concatenate([snapshots, partner], 1).astype(jnp.float32) * cell_weight[:, None]).astype(
        jnp.bfloat16
    )
    begun = local(
        lambda *refs: gram_begin_kernel(3, *refs),
        shape((6, 4, 64, 128), jnp.bfloat16),
        one,
        two,
        one_other,
        weighted,
        name="gram_begin",
        flops=HIDE,
    )
    two_other, begun = lax.optimization_barrier((two_other, begun))
    parts = local(
        gram_end_kernel, shape((16, 2, 64, 128), jnp.bfloat16), two_other, weighted, begun, name="gram_end"
    )
    parts = lax.all_to_all(parts, ("yl", "zl", "yh"), 0, 0, tiled=True)
    parts = local(lambda *refs: sum_kernel(scaling, *refs), shape((4, 64, 128), jnp.float32), parts, name="sum_y")
    parts, one, two, one_other, two_other, time_index, eigvec = lax.optimization_barrier(
        (parts, one, two, one_other, two_other, time_index, eigvec)
    )
    parts = lax.all_to_all(parts, "zh", 0, 0, tiled=True)
    ordered = local(
        ordered_kernel, shape((2, 4, 32, 128), jnp.bfloat16), time_index.reshape(16, 128), eigvec, name="ordered"
    )
    half = shape((16, rows), jnp.float32)
    blocks = one, two, one_other, two_other
    away, stay = local(modes_kernel, [half, half], *blocks, ordered, name="mode_parts")
    away = lax.ppermute(away, "yl", SWAP)
    outs = [shape((64, 128), jnp.float32), half]
    gram, modes = local(last_kernel, outs, parts, stay, away, name="sum_z")
    return gram, modes


def solution(mesh):
    fine = Mesh(mesh.devices.reshape(2, 4, 2, 4, 2, 4), ("yl", "x", "core", "zh", "zl", "yh"))
    snap, space = ("yl", "x", "core"), ("zh", "zl", "yh")
    in_specs = (P(space, snap), P(space), P(), P())
    out_specs = (P(space, snap), P(snap, space))
    return jax.shard_map(body, mesh=fine, in_specs=in_specs, out_specs=out_specs, check_vma=False)
```

```python
import jax
import jax.numpy as jnp
from jax import lax
from jax.experimental import pallas as pl
from jax.experimental.pallas import tpu as pltpu
from jax.sharding import Mesh, PartitionSpec as P

SWAP = [(0, 1), (1, 0)]
HIDE = 20 * 10**9
VMEM = pl.BlockSpec(memory_space=pltpu.VMEM)


def local(kernel, out_shape, *operands, name, flops=0):
    outs = jax.tree.map(lambda _: VMEM, out_shape)
    return pl.pallas_call(
        kernel,
        out_shape=out_shape,
        in_specs=[VMEM] * len(operands),
        out_specs=outs,
        compiler_params=pltpu.CompilerParams(vmem_limit_bytes=32 * 1024 * 1024),
        cost_estimate=pl.CostEstimate(flops=flops, bytes_accessed=0, transcendentals=0) if flops else None,
        name=name,
    )(*operands)


def ordered_kernel(index_ref, eigvec_ref, out_ref):
    y, x, core = lax.axis_index("yl"), lax.axis_index("x"), lax.axis_index("core")
    times, modes = eigvec_ref.shape
    row = lax.broadcasted_iota(jnp.int32, (32, modes), 0)
    column = lax.broadcasted_iota(jnp.int32, (32, modes), 1)
    wanted = (row // 16) * 128 + (x * 2 + core) * 16 + row % 16
    chosen = (column == wanted).astype(jnp.float32).astype(jnp.bfloat16)
    kept = lax.dot_general(
        chosen, eigvec_ref[...], (((1,), (1,)), ((), ())), preferred_element_type=jnp.float32
    ).astype(jnp.bfloat16)
    time = lax.broadcasted_iota(jnp.int32, (times, 128), 0)
    for x1 in range(4):
        for core1 in range(2):
            index = index_ref[pl.ds(y * 8 + x1 * 2 + core1, 1), :]
            hot = (time == index).astype(jnp.float32).astype(jnp.bfloat16)
            out_ref[core1, x1] = jnp.dot(kept, hot, preferred_element_type=jnp.float32).astype(jnp.bfloat16)


def shifts():
    x = lax.axis_index("x")
    return x, (x + 2) % 4, x + 1 - x % 2 * 2, 3 - x


def stack_kernel(first_ref, second_ref, out_ref):
    out_ref[0], out_ref[1] = first_ref[...], second_ref[...]


def gram_blocks(pair_ref, weighted_ref, store):
    weighted = weighted_ref[...]
    for k in range(2):
        part = lax.dot_general(
            pair_ref[k], weighted, (((0,), (0,)), ((), ())), preferred_element_type=jnp.float32
        ).astype(jnp.bfloat16)
        for side in range(2):
            for half in range(2):
                store(k, side * 2 + half, part[half * 64 : half * 64 + 64, side * 128 : side * 128 + 128])


def gram_begin_kernel(pairs, *refs):
    *pair_refs, weighted_ref, out_ref = refs
    for pair in range(pairs):

        def store(k, corner, tile):
            out_ref[pair * 2 + k, corner] = tile

        gram_blocks(pair_refs[pair], weighted_ref, store)


def gram_end_kernel(last_ref, weighted_ref, begun_ref, out_ref):
    y, core = lax.axis_index("yl"), lax.axis_index("core")
    places = shifts()

    def store(k, corner, tile):
        y2, core1, x1 = (y, 1 - y)[corner // 2], (core, 1 - core)[k // 4], places[k % 4]
        out_ref[(core1 * 2 + corner % 2) * 4 + x1 % 2 * 2 + y2, x1 // 2] = tile

    for k in range(6):
        for corner in range(4):
            store(k, corner, begun_ref[k, corner])
    gram_blocks(last_ref, weighted_ref, lambda k, corner, tile: store(6 + k, corner, tile))


def modes_kernel(one_ref, two_ref, one_other_ref, two_other_ref, ordered_ref, away_ref, stay_ref):
    core, places = lax.axis_index("core"), shifts()
    total = jnp.zeros((32, stay_ref.shape[1]), jnp.float32)
    for refs, core1 in (((one_ref, two_ref), core), ((one_other_ref, two_other_ref), 1 - core)):
        for k, x1 in enumerate(places):
            total += lax.dot_general(
                ordered_ref[core1, x1], refs[k // 2][k % 2], (((1,), (1,)), ((), ())), preferred_element_type=jnp.float32
            )
    first = lax.axis_index("yl") == 0
    stay_ref[...] = jnp.where(first, total[:16], total[16:])
    away_ref[...] = jnp.where(first, total[16:], total[:16])


def sum_kernel(scaling, parts_ref, out_ref):
    for y1 in range(2):
        for high in range(2):
            total = parts_ref[y1, high].astype(jnp.float32)
            for k in range(1, 8):
                total += parts_ref[k * 2 + y1, high].astype(jnp.float32)
            out_ref[y1 * 2 + high] = total * scaling


def last_kernel(parts_ref, stay_ref, away_ref, gram_ref, modes_ref):
    total = parts_ref[0]
    for k in range(1, 4):
        total += parts_ref[k]
    gram_ref[...] = total
    modes_ref[...] = stay_ref[...] + away_ref[...]


def body(snapshots, cell_weight, eigvec, time_index):
    rows, width = snapshots.shape
    scaling = 1.0 / (rows * lax.axis_size("zh") * lax.axis_size("zl") * lax.axis_size("yh"))
    shape = jax.ShapeDtypeStruct

    def trade(k):
        return lax.ppermute(snapshots, "x", [(i, i ^ k) for i in range(4)])

    across, ahead, behind = trade(2), trade(1), trade(3)
    partner = lax.ppermute(snapshots, "yl", SWAP)
    pair = shape((2, rows, width), jnp.bfloat16)
    one = local(stack_kernel, pair, snapshots, across, name="stack_one")
    one_other = lax.ppermute(one, "core", SWAP)
    two = local(stack_kernel, pair, ahead, behind, name="stack_two", flops=HIDE)
    two_other = lax.ppermute(two, "core", SWAP)
    weighted = (jnp.concatenate([snapshots, partner], 1).astype(jnp.float32) * cell_weight[:, None]).astype(
        jnp.bfloat16
    )
    begun = local(
        lambda *refs: gram_begin_kernel(3, *refs),
        shape((6, 4, 64, 128), jnp.bfloat16),
        one,
        two,
        one_other,
        weighted,
        name="gram_begin",
        flops=HIDE,
    )
    two_other, begun = lax.optimization_barrier((two_other, begun))
    parts = local(
        gram_end_kernel, shape((16, 2, 64, 128), jnp.bfloat16), two_other, weighted, begun, name="gram_end"
    )
    parts = lax.all_to_all(parts, ("yh", "zl", "yl"), 0, 0, tiled=True)
    parts = local(lambda *refs: sum_kernel(scaling, *refs), shape((4, 64, 128), jnp.float32), parts, name="sum_y")
    parts, one, two, one_other, two_other, time_index, eigvec = lax.optimization_barrier(
        (parts, one, two, one_other, two_other, time_index, eigvec)
    )
    parts = lax.all_to_all(parts, "zh", 0, 0, tiled=True)
    ordered = local(
        ordered_kernel, shape((2, 4, 32, 128), jnp.bfloat16), time_index.reshape(16, 128), eigvec, name="ordered"
    )
    half = shape((16, rows), jnp.float32)
    blocks = one, two, one_other, two_other
    away, stay = local(modes_kernel, [half, half], *blocks, ordered, name="mode_parts")
    away = lax.ppermute(away, "yl", SWAP)
    outs = [shape((64, 128), jnp.float32), half]
    gram, modes = local(last_kernel, outs, parts, stay, away, name="sum_z")
    return gram, modes


def solution(mesh):
    fine = Mesh(mesh.devices.reshape(2, 4, 2, 4, 2, 4), ("yl", "x", "core", "zh", "zl", "yh"))
    snap, space = ("yl", "x", "core"), ("zh", "zl", "yh")
    in_specs = (P(space, snap), P(space), P(), P())
    out_specs = (P(space, snap), P(snap, space))
    return jax.shard_map(body, mesh=fine, in_specs=in_specs, out_specs=out_specs, check_vma=False)
```

```python
import jax
import jax.numpy as jnp
from jax import lax
from jax.experimental import pallas as pl
from jax.experimental.pallas import tpu as pltpu
from jax.sharding import Mesh, PartitionSpec as P

SWAP = [(0, 1), (1, 0)]
SPACE = ("z2", "z1", "zl", "yh1", "yh0")
HIDE = 20 * 10**9
VMEM = pl.BlockSpec(memory_space=pltpu.VMEM)


def local(kernel, out_shape, *operands, name, flops=0):
    outs = jax.tree.map(lambda _: VMEM, out_shape)
    return pl.pallas_call(
        kernel,
        out_shape=out_shape,
        in_specs=[VMEM] * len(operands),
        out_specs=outs,
        compiler_params=pltpu.CompilerParams(vmem_limit_bytes=32 * 1024 * 1024),
        cost_estimate=pl.CostEstimate(flops=flops, bytes_accessed=0, transcendentals=0) if flops else None,
        name=name,
    )(*operands)


def ordered_kernel(index_ref, eigvec_ref, out_ref):
    y, x, core = lax.axis_index("yl"), lax.axis_index("x"), lax.axis_index("core")
    times, modes = eigvec_ref.shape
    row = lax.broadcasted_iota(jnp.int32, (32, modes), 0)
    column = lax.broadcasted_iota(jnp.int32, (32, modes), 1)
    wanted = (row // 16) * 128 + (x * 2 + core) * 16 + row % 16
    chosen = (column == wanted).astype(jnp.float32).astype(jnp.bfloat16)
    kept = lax.dot_general(
        chosen, eigvec_ref[...], (((1,), (1,)), ((), ())), preferred_element_type=jnp.float32
    ).astype(jnp.bfloat16)
    time = lax.broadcasted_iota(jnp.int32, (times, 128), 0)
    for x1 in range(4):
        for core1 in range(2):
            index = index_ref[pl.ds(y * 8 + x1 * 2 + core1, 1), :]
            hot = (time == index).astype(jnp.float32).astype(jnp.bfloat16)
            out_ref[core1, x1] = jnp.dot(kept, hot, preferred_element_type=jnp.float32).astype(jnp.bfloat16)


def shifts():
    x = lax.axis_index("x")
    return x, (x + 2) % 4, x + 1 - x % 2 * 2, 3 - x


def stack_kernel(first_ref, second_ref, out_ref):
    out_ref[0], out_ref[1] = first_ref[...], second_ref[...]


def gram_blocks(pair_ref, weighted_ref, store):
    weighted = weighted_ref[...]
    for k in range(2):
        part = lax.dot_general(
            pair_ref[k], weighted, (((0,), (0,)), ((), ())), preferred_element_type=jnp.float32
        ).astype(jnp.bfloat16)
        for side in range(2):
            for half in range(2):
                store(k, side * 2 + half, part[half * 64 : half * 64 + 64, side * 128 : side * 128 + 128])


def gram_begin_kernel(pairs, *refs):
    *pair_refs, weighted_ref, out_ref = refs
    for pair in range(pairs):

        def store(k, corner, tile):
            out_ref[pair * 2 + k, corner] = tile

        gram_blocks(pair_refs[pair], weighted_ref, store)


def gram_end_kernel(last_ref, weighted_ref, begun_ref, out_ref):
    y, core = lax.axis_index("yl"), lax.axis_index("core")
    places = shifts()

    def store(k, corner, tile):
        y2, core1, x1 = (y, 1 - y)[corner // 2], (core, 1 - core)[k // 4], places[k % 4]
        out_ref[x1 % 2 * 8 + corner % 2 * 4 + core1 * 2 + y2, x1 // 2] = tile

    for k in range(6):
        for corner in range(4):
            store(k, corner, begun_ref[k, corner])
    gram_blocks(last_ref, weighted_ref, lambda k, corner, tile: store(6 + k, corner, tile))


def modes_kernel(one_ref, two_ref, one_other_ref, two_other_ref, ordered_ref, away_ref, stay_ref):
    core, places = lax.axis_index("core"), shifts()
    total = jnp.zeros((32, stay_ref.shape[1]), jnp.float32)
    for refs, core1 in (((one_ref, two_ref), core), ((one_other_ref, two_other_ref), 1 - core)):
        for k, x1 in enumerate(places):
            total += lax.dot_general(
                ordered_ref[core1, x1], refs[k // 2][k % 2], (((1,), (1,)), ((), ())), preferred_element_type=jnp.float32
            )
    first = lax.axis_index("yl") == 0
    stay_ref[...] = jnp.where(first, total[:16], total[16:])
    away_ref[...] = jnp.where(first, total[16:], total[:16])


def sum_kernel(scaling, parts_ref, out_ref):
    for y1 in range(2):
        for high in range(2):
            total = parts_ref[y1, high].astype(jnp.float32)
            for k in range(1, 8):
                total += parts_ref[k * 2 + y1, high].astype(jnp.float32)
            out_ref[high * 2 + y1] = total * scaling


def last_kernel(parts_ref, stay_ref, away_ref, gram_ref, modes_ref):
    total = parts_ref[0]
    for k in range(1, 4):
        total += parts_ref[k]
    gram_ref[...] = total
    modes_ref[...] = stay_ref[...] + away_ref[...]


def body(snapshots, cell_weight, eigvec, time_index):
    rows, width = snapshots.shape
    scaling = 1.0 / (rows * lax.axis_size(SPACE))
    shape = jax.ShapeDtypeStruct

    def trade(k):
        return lax.ppermute(snapshots, "x", [(i, i ^ k) for i in range(4)])

    across, ahead, behind = trade(2), trade(1), trade(3)
    partner = lax.ppermute(snapshots, "yl", SWAP)
    pair = shape((2, rows, width), jnp.bfloat16)
    one = local(stack_kernel, pair, snapshots, across, name="stack_one")
    one_other = lax.ppermute(one, "core", SWAP)
    two = local(stack_kernel, pair, ahead, behind, name="stack_two", flops=HIDE)
    two_other = lax.ppermute(two, "core", SWAP)
    weighted = (jnp.concatenate([snapshots, partner], 1).astype(jnp.float32) * cell_weight[:, None]).astype(
        jnp.bfloat16
    )
    begun = local(
        lambda *refs: gram_begin_kernel(3, *refs),
        shape((6, 4, 64, 128), jnp.bfloat16),
        one,
        two,
        one_other,
        weighted,
        name="gram_begin",
        flops=HIDE,
    )
    two_other, begun = lax.optimization_barrier((two_other, begun))
    parts = local(
        gram_end_kernel, shape((16, 2, 64, 128), jnp.bfloat16), two_other, weighted, begun, name="gram_end"
    )
    parts = lax.all_to_all(parts, ("zl", "yh0", "yh1", "yl"), 0, 0, tiled=True)
    parts = local(lambda *refs: sum_kernel(scaling, *refs), shape((4, 64, 128), jnp.float32), parts, name="sum_y")
    parts, one, two, one_other, two_other, time_index, eigvec = lax.optimization_barrier(
        (parts, one, two, one_other, two_other, time_index, eigvec)
    )
    parts = lax.all_to_all(parts, ("z1", "z2"), 0, 0, tiled=True)
    ordered = local(
        ordered_kernel, shape((2, 4, 32, 128), jnp.bfloat16), time_index.reshape(16, 128), eigvec, name="ordered"
    )
    half = shape((16, rows), jnp.float32)
    blocks = one, two, one_other, two_other
    away, stay = local(modes_kernel, [half, half], *blocks, ordered, name="mode_parts")
    away = lax.ppermute(away, "yl", SWAP)
    outs = [shape((64, 128), jnp.float32), half]
    gram, modes = local(last_kernel, outs, parts, stay, away, name="sum_z")
    return gram, modes


def solution(mesh):
    fine = Mesh(mesh.devices.reshape(2, 4, 2, 2, 2, 2, 2, 2), ("yl", "x", "core") + SPACE)
    snap, space = ("yl", "x", "core"), SPACE
    in_specs = (P(space, snap), P(space), P(), P())
    out_specs = (P(space, snap), P(snap, space))
    return jax.shard_map(body, mesh=fine, in_specs=in_specs, out_specs=out_specs, check_vma=False)
```

```python
import jax
import jax.numpy as jnp
from jax import lax
from jax.experimental import pallas as pl
from jax.experimental.pallas import tpu as pltpu
from jax.sharding import Mesh, PartitionSpec as P

SWAP = [(0, 1), (1, 0)]
SPACE = ("z2", "z1", "zl", "yh1", "yh0")
HIDE = 20 * 10**9
VMEM = pl.BlockSpec(memory_space=pltpu.VMEM)


def local(kernel, out_shape, *operands, name, flops=0):
    outs = jax.tree.map(lambda _: VMEM, out_shape)
    return pl.pallas_call(
        kernel,
        out_shape=out_shape,
        in_specs=[VMEM] * len(operands),
        out_specs=outs,
        compiler_params=pltpu.CompilerParams(vmem_limit_bytes=32 * 1024 * 1024),
        cost_estimate=pl.CostEstimate(flops=flops, bytes_accessed=0, transcendentals=0) if flops else None,
        name=name,
    )(*operands)


def ordered_kernel(index_ref, eigvec_ref, out_ref):
    y, x, core = lax.axis_index("yl"), lax.axis_index("x"), lax.axis_index("core")
    times, modes = eigvec_ref.shape
    row = lax.broadcasted_iota(jnp.int32, (32, modes), 0)
    column = lax.broadcasted_iota(jnp.int32, (32, modes), 1)
    wanted = (row // 16) * 128 + (x * 2 + core) * 16 + row % 16
    chosen = (column == wanted).astype(jnp.float32).astype(jnp.bfloat16)
    kept = lax.dot_general(
        chosen, eigvec_ref[...], (((1,), (1,)), ((), ())), preferred_element_type=jnp.float32
    ).astype(jnp.bfloat16)
    time = lax.broadcasted_iota(jnp.int32, (times, 128), 0)
    for x1 in range(4):
        for core1 in range(2):
            index = index_ref[pl.ds(y * 8 + x1 * 2 + core1, 1), :]
            hot = (time == index).astype(jnp.float32).astype(jnp.bfloat16)
            out_ref[core1, x1] = jnp.dot(kept, hot, preferred_element_type=jnp.float32).astype(jnp.bfloat16)


def shifts():
    x = lax.axis_index("x")
    return x, (x + 2) % 4, x + 1 - x % 2 * 2, 3 - x


def stack_kernel(first_ref, second_ref, out_ref):
    out_ref[0], out_ref[1] = first_ref[...], second_ref[...]


def gram_blocks(pair_ref, weighted_ref, store):
    weighted = weighted_ref[...]
    for k in range(2):
        part = lax.dot_general(
            pair_ref[k], weighted, (((0,), (0,)), ((), ())), preferred_element_type=jnp.float32
        ).astype(jnp.bfloat16)
        for side in range(2):
            for half in range(2):
                store(k, side * 2 + half, part[half * 64 : half * 64 + 64, side * 128 : side * 128 + 128])


def gram_begin_kernel(pairs, *refs):
    *pair_refs, weighted_ref, out_ref = refs
    for pair in range(pairs):

        def store(k, corner, tile):
            out_ref[pair * 2 + k, corner] = tile

        gram_blocks(pair_refs[pair], weighted_ref, store)


def gram_end_kernel(last_ref, weighted_ref, begun_ref, out_ref):
    y, core = lax.axis_index("yl"), lax.axis_index("core")
    places = shifts()

    def store(k, corner, tile):
        y2, core1, x1 = (y, 1 - y)[corner // 2], (core, 1 - core)[k // 4], places[k % 4]
        out_ref[x1 % 2 * 8 + corner % 2 * 4 + core1 * 2 + y2, x1 // 2] = tile

    for k in range(6):
        for corner in range(4):
            store(k, corner, begun_ref[k, corner])
    gram_blocks(last_ref, weighted_ref, lambda k, corner, tile: store(6 + k, corner, tile))


def modes_kernel(keeper, one_ref, two_ref, one_other_ref, two_other_ref, ordered_ref, out_ref):
    y, core, places = lax.axis_index("yl"), lax.axis_index("core"), shifts()
    kept = pl.ds(((y + keeper) % 2) * 16, 16)
    total = jnp.zeros(out_ref.shape, jnp.float32)
    for refs, core1 in (((one_ref, two_ref), core), ((one_other_ref, two_other_ref), 1 - core)):
        for k, x1 in enumerate(places):
            total += lax.dot_general(
                ordered_ref[core1, x1, kept],
                refs[k // 2][k % 2],
                (((1,), (1,)), ((), ())),
                preferred_element_type=jnp.float32,
            )
    out_ref[...] = total


def sum_kernel(scaling, parts_ref, out_ref):
    for y1 in range(2):
        for high in range(2):
            total = parts_ref[y1, high].astype(jnp.float32)
            for k in range(1, 8):
                total += parts_ref[k * 2 + y1, high].astype(jnp.float32)
            out_ref[high * 2 + y1] = total * scaling


def last_kernel(parts_ref, stay_ref, away_ref, gram_ref, modes_ref):
    total = parts_ref[0]
    for k in range(1, 4):
        total += parts_ref[k]
    gram_ref[...] = total
    modes_ref[...] = stay_ref[...] + away_ref[...]


def body(snapshots, cell_weight, eigvec, time_index):
    rows, width = snapshots.shape
    scaling = 1.0 / (rows * lax.axis_size(SPACE))
    shape = jax.ShapeDtypeStruct

    def trade(k):
        return lax.ppermute(snapshots, "x", [(i, i ^ k) for i in range(4)])

    across, ahead, behind = trade(2), trade(1), trade(3)
    partner = lax.ppermute(snapshots, "yl", SWAP)
    pair = shape((2, rows, width), jnp.bfloat16)
    one = local(stack_kernel, pair, snapshots, across, name="stack_one")
    one_other = lax.ppermute(one, "core", SWAP)
    two = local(stack_kernel, pair, ahead, behind, name="stack_two", flops=HIDE)
    two_other = lax.ppermute(two, "core", SWAP)
    weighted = (jnp.concatenate([snapshots, partner], 1).astype(jnp.float32) * cell_weight[:, None]).astype(
        jnp.bfloat16
    )
    begun = local(
        lambda *refs: gram_begin_kernel(3, *refs),
        shape((6, 4, 64, 128), jnp.bfloat16),
        one,
        two,
        one_other,
        weighted,
        name="gram_begin",
        flops=HIDE,
    )
    two_other, begun = lax.optimization_barrier((two_other, begun))
    parts = local(
        gram_end_kernel, shape((16, 2, 64, 128), jnp.bfloat16), two_other, weighted, begun, name="gram_end"
    )
    parts = lax.all_to_all(parts, ("zl", "yh0", "yh1", "yl"), 0, 0, tiled=True)
    parts = local(lambda *refs: sum_kernel(scaling, *refs), shape((4, 64, 128), jnp.float32), parts, name="sum_y")
    parts, one, two, one_other, two_other, time_index, eigvec = lax.optimization_barrier(
        (parts, one, two, one_other, two_other, time_index, eigvec)
    )
    parts = lax.all_to_all(parts, ("z1", "z2"), 0, 0, tiled=True)
    ordered = local(
        ordered_kernel, shape((2, 4, 32, 128), jnp.bfloat16), time_index.reshape(16, 128), eigvec, name="ordered"
    )
    half = shape((16, rows), jnp.float32)
    blocks = one, two, one_other, two_other
    away = local(lambda *refs: modes_kernel(1, *refs), half, *blocks, ordered, name="modes_away")
    away, ordered = lax.optimization_barrier((away, ordered))
    away = lax.ppermute(away, "yl", SWAP)
    stay = local(lambda *refs: modes_kernel(0, *refs), half, *blocks, ordered, name="modes_stay")
    outs = [shape((64, 128), jnp.float32), half]
    gram, modes = local(last_kernel, outs, parts, stay, away, name="sum_z")
    return gram, modes


def solution(mesh):
    fine = Mesh(mesh.devices.reshape(2, 4, 2, 2, 2, 2, 2, 2), ("yl", "x", "core") + SPACE)
    snap, space = ("yl", "x", "core"), SPACE
    in_specs = (P(space, snap), P(space), P(), P())
    out_specs = (P(space, snap), P(snap, space))
    return jax.shard_map(body, mesh=fine, in_specs=in_specs, out_specs=out_specs, check_vma=False)
```
